32 devices in a mesh: rx: 4 (over x, core), ry: 8 (over z, y).
Axes of the slice: x: 2, y: 2, z: 4, core: 2. Of those that a mesh axis runs over, the one named last changes fastest.
Arguments:
- noisy_input: bfloat16 [36864, 12, 128], P(('rx', 'ry')), may hold values from -6 to 6
- adjacency: bfloat16 [288, 6, 128, 128], P(('rx', 'ry')), may hold values from -0.21875 to 0.21875
- neighbours: int32 [288, 6], P(('rx', 'ry')), may hold values from 0 to 8, as said below
- norm_gain: float32 [128], replicated, may hold values from 0.1 to 1.9
- w_mix: bfloat16 [128, 128], replicated, may hold values from -0.5 to 0.5
- pool_weight: bfloat16 [36864], P(('rx', 'ry')), may hold values from 0.049804688 to 0.29882812
- cluster: int32 [36864], P(('rx', 'ry')), may hold values from 0 to 143, as said below
- owner_ids: int32 [4608, 1], P(('rx', 'ry')), may hold values from 0 to 31; in each aligned block of 144 rows (0 to 143, 144 to 287, ...) at most 9 rows name the same one
- w_coarse: bfloat16 [128, 128], replicated, may hold values from -0.5 to 0.5
- w_region: bfloat16 [128, 128], replicated, may hold values from -0.5 to 0.5
- w_out: bfloat16 [128, 128], replicated, may hold values from -0.5 to 0.5
Outputs:
- denoised: bfloat16 [36864, 12, 128], P(('rx', 'ry'))
The draws below stay inside these ranges and needn't reach their ends.
Inputs may be any that keep to these rules, and one draw needn't show every extreme that they name: `neighbours`: the 6 codes of one block are different. `cluster`: among the 1152 nodes of one device's square each value is taken by exactly 8 nodes. `owner_ids`: in each aligned block of 144 rows no value is named by more than 9 rows, and one value is named by exactly 9 rows in some or all blocks; every value is named by some row.
All inputs are finite; a program needn't handle non-finite values.
Results may differ from the reference program's by a relative error of at most 0.015.
Values may be sent and summed in bfloat16 or wider, within the bound.
A program may use at most 128 MiB of HBM per device.

```python
import math
import jax
import jax.numpy as jnp
import numpy as np
from jax import lax

GB = 3
BLK = 128
NB = 6
STEPS = 12
C = 128
ROWS_DEV = 1152
CROWS_DEV = 144
CAP = 9
NODES = 36864
BLOCKS = 288
COARSE = 4608
N_RX = 4
N_RY = 8
DEVICES = 32


def draw_neighbours(key, part):
    ranking = jax.random.randint(key, (BLOCKS, 9), 0, 1 << 20) * 16 + jnp.arange(9, dtype=jnp.int32)[None, :]
    ordering = jnp.argsort(ranking, axis=1, stable=True)
    return ordering[:, :NB].astype(jnp.int32)


def shuffle_one(subkey):
    return jax.random.permutation(subkey, ROWS_DEV)


def draw_cluster(key, part):
    subkeys = jax.random.split(key, NODES // ROWS_DEV)
    shuffled = jax.vmap(shuffle_one)(subkeys)
    return (shuffled // 8).reshape(NODES).astype(jnp.int32)


def block_levels(key, extent, pieces, least, high):
    factor_of, own = 1.0, jax.random.fold_in(key, 6)
    for dim, blocks in pieces:
        draws = jnp.exp(jax.random.uniform(jax.random.fold_in(own, dim), (blocks,), jnp.float32, least / len(pieces), high / len(pieces)))
        factor_of = factor_of * jnp.repeat(draws, extent[dim] // blocks).reshape([-1 if axis == dim else 1 for axis in range(len(extent))])
    return factor_of


def shared_out(rng, own, number, rows, count, top, limit, slope):
    sequence = jax.random.permutation(rng, count)
    heavy_load, common = shares(count, rows * top, limit, slope, True), shares(count, rows * top, limit, slope, False)
    places = jnp.arange(count)

    def named(tallies, offset_by):
        used = int((tallies > 0).sum())
        fixed = max(1, used // 4)
        passed = fixed + (places - fixed + offset_by * (used - fixed)) % max(1, count - fixed)
        return jnp.zeros((count,), jnp.int32).at[sequence[jnp.where(places < fixed, places, passed)]].set(jnp.asarray(tallies, jnp.int32))

    tallies = jnp.where(number % 4 == 0, named(heavy_load, number // 4), named(common, number - number // 4 - 1))
    mixed = jax.random.permutation(jax.random.fold_in(own, 3), count)
    source_of, sink = mixed[0:count // 2 * 2:2], mixed[1:count // 2 * 2:2]
    room = jnp.minimum(tallies[source_of] - 1, limit - tallies[sink]) // 2
    room = jnp.where((source_of == sequence[0]) | (sink == sequence[0]) | (tallies[sink] == 0), 0, jnp.maximum(room, 0))
    passed = jax.random.randint(jax.random.fold_in(own, 4), (count // 2,), 0, 1 << 20) % (room + 1)
    tallies = tallies.at[source_of].add(-passed).at[sink].add(passed)
    members = jnp.searchsorted(jnp.cumsum(tallies), jnp.arange(rows * top), side="right").astype(jnp.int32)
    grid = members.reshape(top, rows).T
    grid = grid[jax.random.permutation(jax.random.fold_in(own, 1), rows)]
    offset_by = jax.random.randint(jax.random.fold_in(own, 2), (rows, 1), 0, top)
    return jnp.take_along_axis(grid, (jnp.arange(top)[None, :] + offset_by) % top, axis=1)


def shares(number_of, total, limit, skew, full):
    loads = [(1 << 20) // math.isqrt(standing ** skew) + 1 for standing in range(1, number_of + 1)]
    largest = limit if full else min(limit, max(-(-total // number_of), total * loads[0] // sum(loads)))
    least = 1 if total - largest >= number_of - 1 else 0
    holding, surplus = [largest] + [least] * (number_of - 1), total - largest - least * (number_of - 1)
    while surplus > 0:
        free = [i for i in range(1, number_of) if holding[i] < largest] or [i for i in range(1, number_of) if holding[i] < limit]
        mass, budget = sum([loads[i] for i in free]), surplus
        for i in free:
            addition = min(limit - holding[i], max(1, budget * loads[i] // mass), surplus)
            holding[i] = holding[i] + addition
            surplus = surplus - addition
    return np.array(holding)


def gaussian(key, shape, width, limit, cuts=(), held_as=jnp.bfloat16):
    loudness = block_levels(key, shape, cuts, -0.22, 0.18) if cuts else 1.0
    drawn = jax.random.normal(key, shape, jnp.float32) * width * loudness
    return jnp.minimum(jnp.maximum(drawn, -limit), limit).astype(held_as)


def setup_inputs(seed: int = 0) -> dict:
    splits = jax.random.split(jax.random.key(seed), 12)
    noisy_input = gaussian(splits[0], (NODES, STEPS, C), 1.0, 6.0, ((0, 32),))
    adjacency = gaussian(splits[1], (BLOCKS, NB, BLK, BLK), (NB * BLK) ** -0.5, 0.21875, ((0, 32),))
    neighbours = draw_neighbours(jax.random.fold_in(splits[11], 71), 0)
    norm_gain = jnp.clip(1.0 + 0.18 * jax.random.normal(splits[3], (C,), jnp.float32), 0.1, 1.9)
    w_mix = gaussian(splits[4], (C, C), C ** -0.5, 0.5)
    pool_weight = jnp.clip(jnp.exp(math.log(0.29882812) - 1.7917595 * jax.random.uniform(splits[5], (NODES,), jnp.float32) ** block_levels(splits[5], (NODES,), ((0, 32),), -0.2, 0.2)), 0.049804688, 0.29882812).astype(jnp.bfloat16)
    cluster = draw_cluster(jax.random.fold_in(splits[11], 71), 0)
    owner_ids_keys = jax.random.split(jax.random.fold_in(splits[7], 1), COARSE // CROWS_DEV)
    owner_ids_turns = jax.random.permutation(jax.random.fold_in(splits[7], 3), COARSE // CROWS_DEV)
    owner_ids = jax.vmap(lambda own, number: shared_out(jax.random.fold_in(splits[7], 2), own, number, CROWS_DEV, DEVICES, 1, CAP, 2))(owner_ids_keys, owner_ids_turns).reshape((COARSE, 1))
    w_coarse = gaussian(splits[8], (C, C), C ** -0.5, 0.5)
    w_region = gaussian(splits[9], (C, C), C ** -0.5, 0.5)
    w_out = gaussian(splits[10], (C, C), C ** -0.5, 0.5)
    return dict(noisy_input=noisy_input, adjacency=adjacency, neighbours=neighbours, norm_gain=norm_gain, w_mix=w_mix, pool_weight=pool_weight, cluster=cluster, owner_ids=owner_ids, w_coarse=w_coarse, w_region=w_region, w_out=w_out)


def diffuse(values_in, adjacency, offsets):
    features = STEPS * C
    grid_blocks = values_in.reshape(N_RX, N_RY, GB, GB, BLK, features)
    grid_blocks = grid_blocks.transpose(0, 2, 1, 3, 4, 5).reshape(N_RX * GB, N_RY * GB, BLK, features)
    padded = jnp.pad(grid_blocks, ((1, 1), (1, 1), (0, 0), (0, 0)))
    local_weights = adjacency.reshape(DEVICES, GB * GB, NB, BLK, BLK)
    local_offsets = offsets.reshape(DEVICES, GB * GB, NB)
    positions = jnp.arange(GB * GB, dtype=jnp.int32)

    def one_device(carried):
        device_id, weights, offset_codes = carried
        first_row = device_id // N_RY * GB
        first_col = device_id % N_RY * GB
        row_at = first_row + (positions // GB)[:, None] + offset_codes // 3
        col_at = first_col + (positions % GB)[:, None] + offset_codes % 3
        gathered = padded[row_at, col_at]
        return jnp.einsum('bkij,bkjf->bif', weights.astype(jnp.float32), gathered.astype(jnp.float32))
    summed = lax.map(one_device, (jnp.arange(DEVICES, dtype=jnp.int32), local_weights, local_offsets))
    return summed.reshape(NODES, STEPS, C)

def reference(noisy_input, adjacency, neighbours, norm_gain, w_mix, pool_weight, cluster, owner_ids, w_coarse, w_region, w_out):
    diffused = diffuse(noisy_input, adjacency, neighbours).astype(jnp.bfloat16)
    scaled = diffused.astype(jnp.float32)
    mean_square = lax.optimization_barrier(jnp.mean(scaled * scaled, axis=-1, keepdims=True))
    normed = (scaled * lax.rsqrt(mean_square + 1e-06) * norm_gain).astype(jnp.bfloat16)
    mixed = jnp.dot(normed.reshape(-1, C), w_mix, preferred_element_type=jnp.float32).reshape(NODES, STEPS, C)
    encoded = (noisy_input.astype(jnp.float32) + jax.nn.silu(mixed)).astype(jnp.bfloat16)
    coarse_index = jnp.arange(NODES, dtype=jnp.int32) // ROWS_DEV * CROWS_DEV + cluster
    weighted = pool_weight.astype(jnp.float32)[:, None, None] * encoded.astype(jnp.float32)
    pooled = jax.ops.segment_sum(weighted, coarse_index, COARSE).astype(jnp.bfloat16)
    owners = owner_ids[:, 0]
    lifted = jax.nn.silu(jnp.dot(pooled.reshape(-1, C), w_coarse, preferred_element_type=jnp.float32))
    lifted = lifted.astype(jnp.bfloat16).reshape(COARSE, STEPS, C)
    region_sum = jax.ops.segment_sum(lifted.astype(jnp.float32), owners, DEVICES)
    region = (region_sum / float(CROWS_DEV)).astype(jnp.bfloat16)
    reach = jnp.dot(region.reshape(-1, C), w_region, preferred_element_type=jnp.float32).reshape(DEVICES, STEPS, C)
    refined = (pooled.astype(jnp.float32) + lifted.astype(jnp.float32) + reach[owners]).astype(jnp.bfloat16)
    decoder_in = (encoded.astype(jnp.float32) + refined[coarse_index].astype(jnp.float32)).astype(jnp.bfloat16)
    second = diffuse(decoder_in, adjacency, neighbours).astype(jnp.bfloat16)
    output = jnp.dot(second.reshape(-1, C), w_out, preferred_element_type=jnp.float32).reshape(NODES, STEPS, C)
    return (decoder_in.astype(jnp.float32) + jax.nn.silu(output)).astype(jnp.bfloat16)
```

```python
import functools
import jax
import jax.numpy as jnp
from jax import lax
from jax.experimental import pallas as pl
from jax.experimental.pallas import tpu as pltpu
from jax.sharding import PartitionSpec as P

GB = 3
BLK = 128
SIDE = GB + 2
CHUNKS = 2
LANES_STEPS = 2


def silu(v):
    return v / (1.0 + jnp.exp(-v))


def dot32(a, b):
    return jnp.dot(a, b, preferred_element_type=jnp.float32)


def extended_sources(own, rx_lo, rx_hi, ry_lo, ry_hi, co_lo, co_hi):
    sources = []
    for r in range(SIDE):
        for c in range(SIDE):
            if r in (0, SIDE - 1):
                row, corner = (rx_lo, co_lo) if r == 0 else (rx_hi, co_hi)
                if c in (0, SIDE - 1):
                    sources.append((corner, 0 if c == 0 else 1))
                else:
                    sources.append((row, c - 1))
            elif c in (0, SIDE - 1):
                sources.append((ry_lo if c == 0 else ry_hi, r - 1))
            else:
                sources.append((own, (r - 1) * GB + c - 1))
    return sources


def diffuse_block(b, index, adjacency, ext):
    lhs = jnp.concatenate([adjacency[b, n] for n in range(adjacency.shape[1])], axis=1)
    rhs = jnp.concatenate(
        [ext[index[b * adjacency.shape[1] + n]] for n in range(adjacency.shape[1])], axis=0
    )
    return dot32(lhs, rhs)


def encode_kernel(
    index,
    own,
    rx_lo,
    rx_hi,
    ry_lo,
    ry_hi,
    co_lo,
    co_hi,
    adjacency,
    gain,
    w_mix,
    weight_row,
    cluster_row,
    cluster_col,
    owner_row,
    w_coarse,
    u_ref,
    partial_ref,
    ext,
    enc,
):
    steps = own.shape[0]
    coarse = owner_row.shape[1]
    nodes = cluster_row.shape[1]
    devices = partial_ref.shape[1]
    for p, (ref, k) in enumerate(
        extended_sources(own, rx_lo, rx_hi, ry_lo, ry_hi, co_lo, co_hi)
    ):
        for t in range(steps):
            ext[p, :, t * BLK : (t + 1) * BLK] = ref[t, k]
    pooled = jnp.zeros((coarse, steps * BLK), jnp.float32)
    for b in range(GB * GB):
        summed = diffuse_block(b, index, adjacency, ext)
        for t in range(steps):
            scaled = summed[:, t * BLK : (t + 1) * BLK].astype(jnp.bfloat16).astype(jnp.float32)
            mean_square = jnp.mean(scaled * scaled, axis=-1, keepdims=True)
            normed = (scaled * lax.rsqrt(mean_square + 1e-06) * gain[...]).astype(jnp.bfloat16)
            mixed = dot32(normed, w_mix[...])
            enc[b, :, t * BLK : (t + 1) * BLK] = (
                own[t, b].astype(jnp.float32) + silu(mixed)
            ).astype(jnp.bfloat16)
        lanes = slice(b * BLK, (b + 1) * BLK)
        rows = lax.broadcasted_iota(jnp.int32, (coarse, BLK), 0)
        pooling = jnp.where(
            rows == cluster_row[:, lanes], weight_row[:, lanes], 0.0
        ).astype(jnp.bfloat16)
        pooled = pooled + dot32(pooling, enc[b])
    pooled = pooled.astype(jnp.bfloat16)
    owner_hot = (
        lax.broadcasted_iota(jnp.int32, (devices, coarse), 0) == owner_row[...]
    ).astype(jnp.float32).astype(jnp.bfloat16)
    bases = []
    for t in range(steps):
        piece = pooled[:, t * BLK : (t + 1) * BLK]
        lifted = silu(dot32(piece, w_coarse[...])).astype(jnp.bfloat16)
        partial_ref[t] = dot32(owner_hot, lifted)
        bases.append((piece.astype(jnp.float32) + lifted.astype(jnp.float32)).astype(jnp.bfloat16))
    base = jnp.concatenate(bases, axis=1)
    for b in range(GB * GB):
        hot = (
            lax.broadcasted_iota(jnp.int32, (BLK, coarse), 1)
            == cluster_col[b * BLK : (b + 1) * BLK, :]
        ).astype(jnp.float32).astype(jnp.bfloat16)
        u = (enc[b].astype(jnp.float32) + dot32(hot, base)).astype(jnp.bfloat16)
        for t in range(steps):
            u_ref[t, b] = u[:, t * BLK : (t + 1) * BLK]


def decode_kernel(
    denominator,
    index,
    own,
    rx_lo,
    rx_hi,
    ry_lo,
    ry_hi,
    co_lo,
    co_hi,
    adjacency,
    region_sum,
    owner_ext,
    w_region,
    w_out,
    *rest,
):
    out_ref, ext = rest[-2:]
    steps = own.shape[0]
    devices = region_sum.shape[1]
    reaches = []
    for t in range(steps):
        region = (region_sum[t] / denominator).astype(jnp.bfloat16)
        reaches.append(dot32(region, w_region[...]).astype(jnp.bfloat16))
    reach = jnp.concatenate(reaches, axis=1)
    for p, (ref, k) in enumerate(
        extended_sources(own, rx_lo, rx_hi, ry_lo, ry_hi, co_lo, co_hi)
    ):
        hot = (
            lax.broadcasted_iota(jnp.int32, (BLK, devices), 1)
            == owner_ext[p * BLK : (p + 1) * BLK, :]
        ).astype(jnp.float32).astype(jnp.bfloat16)
        added = dot32(hot, reach)
        for t in range(steps):
            lanes = slice(t * BLK, (t + 1) * BLK)
            ext[p, :, lanes] = (ref[t, k].astype(jnp.float32) + added[:, lanes]).astype(
                jnp.bfloat16
            )
    for b in range(GB * GB):
        second = diffuse_block(b, index, adjacency, ext).astype(jnp.bfloat16)
        centre = (b // GB + 1) * SIDE + b % GB + 1
        for t in range(steps):
            lanes = slice(t * BLK, (t + 1) * BLK)
            mixed = dot32(second[:, lanes], w_out[...])
            out_ref[t, b] = (ext[centre, :, lanes].astype(jnp.float32) + silu(mixed)).astype(
                jnp.bfloat16
            )


def stepped(array, per, offset=0):
    tail = array.shape[1:]
    zeros = (0,) * len(tail)
    return pl.BlockSpec((per,) + tail, lambda i, _: (i + offset,) + zeros)


def whole(array):
    zeros = (0,) * array.ndim
    return pl.BlockSpec(array.shape, lambda i, _: zeros)


def halo(field):
    steps = field.shape[0]
    square = field.reshape(steps, GB, GB, BLK, BLK)

    def shifted(value, axis, up):
        count = lax.axis_size(axis)
        pairs = [(i, i + 1) if up else (i + 1, i) for i in range(count - 1)]
        return lax.ppermute(value, axis, pairs)

    ry_lo = shifted(square[:, :, GB - 1], "ry", True)
    ry_hi = shifted(square[:, :, 0], "ry", False)
    rx_lo = shifted(square[:, GB - 1], "rx", True)
    rx_hi = shifted(square[:, 0], "rx", False)
    co_lo = shifted(jnp.stack([ry_lo[:, GB - 1], ry_hi[:, GB - 1]], axis=1), "rx", True)
    co_hi = shifted(jnp.stack([ry_lo[:, 0], ry_hi[:, 0]], axis=1), "rx", False)
    return rx_lo, rx_hi, ry_lo, ry_hi, co_lo, co_hi


def on_device(
    noisy_input,
    adjacency,
    neighbours,
    norm_gain,
    w_mix,
    pool_weight,
    cluster,
    owner_ids,
    w_coarse,
    w_region,
    w_out,
):
    node_rows, steps_count, channels = noisy_input.shape
    coarse = owner_ids.shape[0]
    row_devices = lax.axis_size("rx")
    col_devices = lax.axis_size("ry")
    devices = row_devices * col_devices
    blocks = GB * GB
    noisy = noisy_input.transpose(1, 0, 2).reshape(steps_count, blocks, BLK, channels)
    positions = jnp.arange(blocks, dtype=jnp.int32)
    index = (
        (positions // GB)[:, None] + neighbours // 3
    ) * SIDE + (positions % GB)[:, None] + neighbours % 3
    index = index.reshape(-1)

    targets = owner_ids[:, 0]
    owner_of = jnp.sum(
        jnp.where(
            cluster[:, None] == jnp.arange(coarse, dtype=jnp.int32)[None, :], targets[None, :], 0
        ),
        axis=1,
    )
    everyone = lax.all_gather(owner_of.reshape(blocks, BLK), ("rx", "ry"), axis=0, tiled=True)
    ext_rows = jnp.arange(SIDE * SIDE, dtype=jnp.int32)
    grid_row = lax.axis_index("rx") * GB + ext_rows // SIDE - 1
    grid_col = lax.axis_index("ry") * GB + ext_rows % SIDE - 1
    inside = (
        (grid_row >= 0)
        & (grid_row < row_devices * GB)
        & (grid_col >= 0)
        & (grid_col < col_devices * GB)
    )
    grid_row = jnp.clip(grid_row, 0, row_devices * GB - 1)
    grid_col = jnp.clip(grid_col, 0, col_devices * GB - 1)
    place = (
        (grid_row // GB * col_devices + grid_col // GB) * blocks
        + grid_row % GB * GB
        + grid_col % GB
    )
    owner_ext = jnp.where(inside[:, None], everyone[place], -1).reshape(SIDE * SIDE * BLK, 1)

    chunk = steps_count // CHUNKS
    per = LANES_STEPS
    grid = chunk // per
    gain = norm_gain.reshape(1, channels)
    weight_row = pool_weight.astype(jnp.float32).reshape(1, node_rows)
    cluster_row = cluster.reshape(1, node_rows)
    cluster_col = cluster.reshape(node_rows, 1)
    owner_row = targets.reshape(1, coarse)
    ext_scratch = pltpu.VMEM((SIDE * SIDE, BLK, per * BLK), jnp.bfloat16)
    params = pltpu.CompilerParams(vmem_limit_bytes=48 * 1024 * 1024)
    cost = pl.CostEstimate(flops=5_000_000_000 // CHUNKS, bytes_accessed=16_000_000 // CHUNKS, transcendentals=0)

    first = [halo(noisy[c * chunk : (c + 1) * chunk]) for c in range(CHUNKS)]
    fields, sums, second = [], [], []
    for c in range(CHUNKS):
        constants = (
            adjacency, gain, w_mix, weight_row, cluster_row, cluster_col, owner_row, w_coarse,
        )
        u, partial = pl.pallas_call(
            encode_kernel,
            grid_spec=pltpu.PrefetchScalarGridSpec(
                num_scalar_prefetch=1,
                grid=(grid,),
                in_specs=[stepped(noisy, per, c * grid)]
                + [stepped(part, per) for part in first[c]]
                + [whole(part) for part in constants],
                out_specs=[
                    pl.BlockSpec((per, blocks, BLK, channels), lambda i, _: (i, 0, 0, 0)),
                    pl.BlockSpec((per, devices, channels), lambda i, _: (i, 0, 0)),
                ],
                scratch_shapes=[
                    ext_scratch,
                    pltpu.VMEM((blocks, BLK, per * BLK), jnp.bfloat16),
                ],
            ),
            out_shape=[
                jax.ShapeDtypeStruct((chunk, blocks, BLK, channels), jnp.bfloat16),
                jax.ShapeDtypeStruct((chunk, devices, channels), jnp.float32),
            ],
            compiler_params=params,
            cost_estimate=cost,
            name="encode",
        )(index, noisy, *first[c], *constants)
        fields.append(u)
        sums.append(partial)
        second.append(halo(u))
    region_sum = lax.psum(jnp.concatenate(sums, axis=0), ("rx", "ry"))

    out = None
    for c in range(CHUNKS):
        shared = (owner_ext, w_region, w_out)
        extra = () if out is None else (out,)
        operands = (index, fields[c], *second[c], adjacency, region_sum, *shared, *extra)
        out = pl.pallas_call(
            functools.partial(decode_kernel, float(coarse)),
            grid_spec=pltpu.PrefetchScalarGridSpec(
                num_scalar_prefetch=1,
                grid=(grid,),
                in_specs=[stepped(fields[c], per)]
                + [stepped(part, per) for part in second[c]]
                + [whole(adjacency), stepped(region_sum, per, c * grid)]
                + [whole(part) for part in shared]
                + [pl.BlockSpec(memory_space=pl.ANY)] * len(extra),
                out_specs=pl.BlockSpec(
                    (per, blocks, BLK, channels), lambda i, _, c=c: (i + c * grid, 0, 0, 0)
                ),
                scratch_shapes=[ext_scratch],
            ),
            out_shape=jax.ShapeDtypeStruct((steps_count, blocks, BLK, channels), jnp.bfloat16),
            input_output_aliases={len(operands) - 1: 0} if extra else {},
            compiler_params=params,
            cost_estimate=cost,
            name="decode",
        )(*operands)
    return out.reshape(steps_count, node_rows, channels).transpose(1, 0, 2)


def solution(mesh):
    in_specs = (
        P(("rx", "ry"), None, None),
        P(("rx", "ry"), None, None, None),
        P(("rx", "ry"), None),
        P(),
        P(),
        P(("rx", "ry")),
        P(("rx", "ry")),
        P(("rx", "ry"), None),
        P(),
        P(),
        P(),
    )
    out_specs = P(("rx", "ry"), None, None)
    return jax.shard_map(
        on_device, mesh=mesh, in_specs=in_specs, out_specs=out_specs, check_vma=False
    )
```

```python
import jax
import jax.numpy as jnp
from jax import lax
from jax.experimental import pallas as pl
from jax.experimental.pallas import tpu as pltpu
from jax.sharding import PartitionSpec as P

GB = 3
BLK = 128
SIDE = GB + 2
CHUNKS = 2
LANES_STEPS = 2


def silu(v):
    return v / (1.0 + jnp.exp(-v))


def dot32(a, b):
    return jnp.dot(a, b, preferred_element_type=jnp.float32)


def extended_sources(own, rx_lo, rx_hi, ry_lo, ry_hi, co_lo, co_hi):
    sources = []
    for r in range(SIDE):
        for c in range(SIDE):
            if r in (0, SIDE - 1):
                row, corner = (rx_lo, co_lo) if r == 0 else (rx_hi, co_hi)
                if c in (0, SIDE - 1):
                    sources.append((corner, 0 if c == 0 else 1))
                else:
                    sources.append((row, c - 1))
            elif c in (0, SIDE - 1):
                sources.append((ry_lo if c == 0 else ry_hi, r - 1))
            else:
                sources.append((own, (r - 1) * GB + c - 1))
    return sources


def diffuse_block(b, index, adjacency, ext):
    lhs = jnp.concatenate([adjacency[b, n] for n in range(adjacency.shape[1])], axis=1)
    rhs = jnp.concatenate(
        [ext[index[b * adjacency.shape[1] + n]] for n in range(adjacency.shape[1])], axis=0
    )
    return dot32(lhs, rhs)


def encode_kernel(
    index,
    own,
    rx_lo,
    rx_hi,
    ry_lo,
    ry_hi,
    co_lo,
    co_hi,
    adjacency,
    gain,
    w_mix,
    weight_row,
    cluster_row,
    cluster_col,
    owner_row,
    w_coarse,
    u_ref,
    partial_ref,
    ext,
    enc,
):
    steps = own.shape[0]
    coarse = owner_row.shape[1]
    nodes = cluster_row.shape[1]
    devices = partial_ref.shape[1]
    for p, (ref, k) in enumerate(
        extended_sources(own, rx_lo, rx_hi, ry_lo, ry_hi, co_lo, co_hi)
    ):
        for t in range(steps):
            ext[p, :, t * BLK : (t + 1) * BLK] = ref[t, k]
    pooled = jnp.zeros((coarse, steps * BLK), jnp.float32)
    for b in range(GB * GB):
        summed = diffuse_block(b, index, adjacency, ext)
        for t in range(steps):
            scaled = summed[:, t * BLK : (t + 1) * BLK].astype(jnp.bfloat16).astype(jnp.float32)
            mean_square = jnp.mean(scaled * scaled, axis=-1, keepdims=True)
            normed = (scaled * lax.rsqrt(mean_square + 1e-06) * gain[...]).astype(jnp.bfloat16)
            mixed = dot32(normed, w_mix[...])
            enc[b, :, t * BLK : (t + 1) * BLK] = (
                own[t, b].astype(jnp.float32) + silu(mixed)
            ).astype(jnp.bfloat16)
        lanes = slice(b * BLK, (b + 1) * BLK)
        rows = lax.broadcasted_iota(jnp.int32, (coarse, BLK), 0)
        pooling = jnp.where(
            rows == cluster_row[:, lanes], weight_row[:, lanes], 0.0
        ).astype(jnp.bfloat16)
        pooled = pooled + dot32(pooling, enc[b])
    pooled = pooled.astype(jnp.bfloat16)
    owner_hot = (
        lax.broadcasted_iota(jnp.int32, (devices, coarse), 0) == owner_row[...]
    ).astype(jnp.float32).astype(jnp.bfloat16)
    bases = []
    for t in range(steps):
        piece = pooled[:, t * BLK : (t + 1) * BLK]
        lifted = silu(dot32(piece, w_coarse[...])).astype(jnp.bfloat16)
        partial_ref[t] = dot32(owner_hot, lifted)
        bases.append((piece.astype(jnp.float32) + lifted.astype(jnp.float32)).astype(jnp.bfloat16))
    base = jnp.concatenate(bases, axis=1)
    for b in range(GB * GB):
        hot = (
            lax.broadcasted_iota(jnp.int32, (BLK, coarse), 1)
            == cluster_col[b * BLK : (b + 1) * BLK, :]
        ).astype(jnp.float32).astype(jnp.bfloat16)
        u = (enc[b].astype(jnp.float32) + dot32(hot, base)).astype(jnp.bfloat16)
        for t in range(steps):
            u_ref[t, b] = u[:, t * BLK : (t + 1) * BLK]


def decode_kernel(
    index,
    own,
    rx_lo,
    rx_hi,
    ry_lo,
    ry_hi,
    co_lo,
    co_hi,
    adjacency,
    region,
    owner_ext,
    w_region,
    w_out,
    *rest,
):
    out_ref, ext = rest[-2:]
    steps = own.shape[0]
    devices = region.shape[1]
    reaches = []
    for t in range(steps):
        reaches.append(dot32(region[t], w_region[...]).astype(jnp.bfloat16))
    reach = jnp.concatenate(reaches, axis=1)
    for p, (ref, k) in enumerate(
        extended_sources(own, rx_lo, rx_hi, ry_lo, ry_hi, co_lo, co_hi)
    ):
        hot = (
            lax.broadcasted_iota(jnp.int32, (BLK, devices), 1)
            == owner_ext[p * BLK : (p + 1) * BLK, :]
        ).astype(jnp.float32).astype(jnp.bfloat16)
        added = dot32(hot, reach)
        for t in range(steps):
            lanes = slice(t * BLK, (t + 1) * BLK)
            ext[p, :, lanes] = (ref[t, k].astype(jnp.float32) + added[:, lanes]).astype(
                jnp.bfloat16
            )
    for b in range(GB * GB):
        second = diffuse_block(b, index, adjacency, ext).astype(jnp.bfloat16)
        centre = (b // GB + 1) * SIDE + b % GB + 1
        for t in range(steps):
            lanes = slice(t * BLK, (t + 1) * BLK)
            mixed = dot32(second[:, lanes], w_out[...])
            out_ref[t, b] = (ext[centre, :, lanes].astype(jnp.float32) + silu(mixed)).astype(
                jnp.bfloat16
            )


def stepped(array, per, offset=0):
    tail = array.shape[1:]
    zeros = (0,) * len(tail)
    return pl.BlockSpec((per,) + tail, lambda i, _: (i + offset,) + zeros)


def whole(array):
    zeros = (0,) * array.ndim
    return pl.BlockSpec(array.shape, lambda i, _: zeros)


def shifted(value, axis, up):
    count = lax.axis_size(axis)
    pairs = [(i, i + 1) if up else (i + 1, i) for i in range(count - 1)]
    return lax.ppermute(value, axis, pairs)


def halo(field):
    steps = field.shape[0]
    square = field.reshape(steps, GB, GB, BLK, BLK)

    ry_lo = shifted(square[:, :, GB - 1], "ry", True)
    ry_hi = shifted(square[:, :, 0], "ry", False)
    rx_lo = shifted(square[:, GB - 1], "rx", True)
    rx_hi = shifted(square[:, 0], "rx", False)
    co_lo = shifted(jnp.stack([ry_lo[:, GB - 1], ry_hi[:, GB - 1]], axis=1), "rx", True)
    co_hi = shifted(jnp.stack([ry_lo[:, 0], ry_hi[:, 0]], axis=1), "rx", False)
    return rx_lo, rx_hi, ry_lo, ry_hi, co_lo, co_hi


def on_device(
    noisy_input,
    adjacency,
    neighbours,
    norm_gain,
    w_mix,
    pool_weight,
    cluster,
    owner_ids,
    w_coarse,
    w_region,
    w_out,
):
    node_rows, steps_count, channels = noisy_input.shape
    coarse = owner_ids.shape[0]
    row_devices = lax.axis_size("rx")
    col_devices = lax.axis_size("ry")
    devices = row_devices * col_devices
    blocks = GB * GB
    noisy = noisy_input.transpose(1, 0, 2).reshape(steps_count, blocks, BLK, channels)
    positions = jnp.arange(blocks, dtype=jnp.int32)
    index = (
        (positions // GB)[:, None] + neighbours // 3
    ) * SIDE + (positions % GB)[:, None] + neighbours % 3
    index = index.reshape(-1)

    targets = owner_ids[:, 0]
    owner_of = jnp.sum(
        jnp.where(
            cluster[:, None] == jnp.arange(coarse, dtype=jnp.int32)[None, :], targets[None, :], 0
        ),
        axis=1,
    )
    marks = (owner_of + 1).reshape(GB, GB, BLK)
    marks = jnp.concatenate(
        [shifted(marks[:, -1:], "ry", True), marks, shifted(marks[:, :1], "ry", False)], axis=1
    )
    marks = jnp.concatenate(
        [shifted(marks[-1:], "rx", True), marks, shifted(marks[:1], "rx", False)], axis=0
    )
    owner_ext = (marks - 1).reshape(SIDE * SIDE * BLK, 1)

    chunk = steps_count // CHUNKS
    per = LANES_STEPS
    grid = chunk // per
    gain = norm_gain.reshape(1, channels)
    weight_row = pool_weight.astype(jnp.float32).reshape(1, node_rows)
    cluster_row = cluster.reshape(1, node_rows)
    cluster_col = cluster.reshape(node_rows, 1)
    owner_row = targets.reshape(1, coarse)
    ext_scratch = pltpu.VMEM((SIDE * SIDE, BLK, per * BLK), jnp.bfloat16)
    params = pltpu.CompilerParams(vmem_limit_bytes=48 * 1024 * 1024)
    cost = pl.CostEstimate(flops=5_000_000_000 // CHUNKS, bytes_accessed=16_000_000 // CHUNKS, transcendentals=0)

    first = [halo(noisy[c * chunk : (c + 1) * chunk]) for c in range(CHUNKS)]
    fields, sums, second = [], [], []
    for c in range(CHUNKS):
        constants = (
            adjacency, gain, w_mix, weight_row, cluster_row, cluster_col, owner_row, w_coarse,
        )
        u, partial = pl.pallas_call(
            encode_kernel,
            grid_spec=pltpu.PrefetchScalarGridSpec(
                num_scalar_prefetch=1,
                grid=(grid,),
                in_specs=[stepped(noisy, per, c * grid)]
                + [stepped(part, per) for part in first[c]]
                + [whole(part) for part in constants],
                out_specs=[
                    pl.BlockSpec((per, blocks, BLK, channels), lambda i, _: (i, 0, 0, 0)),
                    pl.BlockSpec((per, devices, channels), lambda i, _: (i, 0, 0)),
                ],
                scratch_shapes=[
                    ext_scratch,
                    pltpu.VMEM((blocks, BLK, per * BLK), jnp.bfloat16),
                ],
            ),
            out_shape=[
                jax.ShapeDtypeStruct((chunk, blocks, BLK, channels), jnp.bfloat16),
                jax.ShapeDtypeStruct((chunk, devices, channels), jnp.float32),
            ],
            compiler_params=params,
            cost_estimate=cost,
            name="encode",
        )(index, noisy, *first[c], *constants)
        fields.append(u)
        sums.append(partial)
        second.append(halo(u))
    mine = lax.all_to_all(
        jnp.concatenate(sums, axis=0).transpose(1, 0, 2),
        ("rx", "ry"),
        split_axis=0,
        concat_axis=0,
        tiled=True,
    )
    own_region = (jnp.sum(mine, axis=0) / float(coarse)).astype(jnp.bfloat16)
    region = lax.all_to_all(
        jnp.broadcast_to(own_region[None], (devices, steps_count, channels)),
        ("rx", "ry"),
        split_axis=0,
        concat_axis=0,
        tiled=True,
    ).transpose(1, 0, 2)

    out = None
    for c in range(CHUNKS):
        shared = (owner_ext, w_region, w_out)
        extra = () if out is None else (out,)
        operands = (index, fields[c], *second[c], adjacency, region, *shared, *extra)
        out = pl.pallas_call(
            decode_kernel,
            grid_spec=pltpu.PrefetchScalarGridSpec(
                num_scalar_prefetch=1,
                grid=(grid,),
                in_specs=[stepped(fields[c], per)]
                + [stepped(part, per) for part in second[c]]
                + [whole(adjacency), stepped(region, per, c * grid)]
                + [whole(part) for part in shared]
                + [pl.BlockSpec(memory_space=pl.ANY)] * len(extra),
                out_specs=pl.BlockSpec(
                    (per, blocks, BLK, channels), lambda i, _, c=c: (i + c * grid, 0, 0, 0)
                ),
                scratch_shapes=[ext_scratch],
            ),
            out_shape=jax.ShapeDtypeStruct((steps_count, blocks, BLK, channels), jnp.bfloat16),
            input_output_aliases={len(operands) - 1: 0} if extra else {},
            compiler_params=params,
            cost_estimate=cost,
            name="decode",
        )(*operands)
    return out.reshape(steps_count, node_rows, channels).transpose(1, 0, 2)


def solution(mesh):
    in_specs = (
        P(("rx", "ry"), None, None),
        P(("rx", "ry"), None, None, None),
        P(("rx", "ry"), None),
        P(),
        P(),
        P(("rx", "ry")),
        P(("rx", "ry")),
        P(("rx", "ry"), None),
        P(),
        P(),
        P(),
    )
    out_specs = P(("rx", "ry"), None, None)
    return jax.shard_map(
        on_device, mesh=mesh, in_specs=in_specs, out_specs=out_specs, check_vma=False
    )
```

```python
import jax
import jax.numpy as jnp
from jax import lax
from jax.experimental import pallas as pl
from jax.experimental.pallas import tpu as pltpu
from jax.sharding import PartitionSpec as P

GB = 3
BLK = 128
SIDE = GB + 2
CHUNKS = 2
LANES_STEPS = 2


def silu(v):
    return v / (1.0 + jnp.exp(-v))


def dot32(a, b):
    return jnp.dot(a, b, preferred_element_type=jnp.float32)


def extended_sources(own, rx_lo, rx_hi, ry_lo, ry_hi, co_lo, co_hi):
    sources = []
    for r in range(SIDE):
        for c in range(SIDE):
            if r in (0, SIDE - 1):
                row, corner = (rx_lo, co_lo) if r == 0 else (rx_hi, co_hi)
                if c in (0, SIDE - 1):
                    sources.append((corner, 0 if c == 0 else 1))
                else:
                    sources.append((row, c - 1))
            elif c in (0, SIDE - 1):
                sources.append((ry_lo if c == 0 else ry_hi, r - 1))
            else:
                sources.append((own, (r - 1) * GB + c - 1))
    return sources


def diffuse_block(b, index, adjacency, ext):
    lhs = jnp.concatenate([adjacency[b, n] for n in range(adjacency.shape[1])], axis=1)
    rhs = jnp.concatenate(
        [ext[index[b * adjacency.shape[1] + n]] for n in range(adjacency.shape[1])], axis=0
    )
    return dot32(lhs, rhs)


def encode_kernel(
    index,
    own,
    rx_lo,
    rx_hi,
    ry_lo,
    ry_hi,
    co_lo,
    co_hi,
    adjacency,
    gain,
    w_mix,
    weight_row,
    cluster_row,
    cluster_col,
    owner_row,
    w_coarse,
    u_ref,
    partial_ref,
    ext,
    enc,
):
    steps = own.shape[0]
    coarse = owner_row.shape[1]
    nodes = cluster_row.shape[1]
    devices = partial_ref.shape[1]
    for p, (ref, k) in enumerate(
        extended_sources(own, rx_lo, rx_hi, ry_lo, ry_hi, co_lo, co_hi)
    ):
        for t in range(steps):
            ext[p, :, t * BLK : (t + 1) * BLK] = ref[t, k]
    pooled = jnp.zeros((coarse, steps * BLK), jnp.float32)
    for b in range(GB * GB):
        summed = diffuse_block(b, index, adjacency, ext)
        for t in range(steps):
            scaled = summed[:, t * BLK : (t + 1) * BLK].astype(jnp.bfloat16).astype(jnp.float32)
            mean_square = jnp.mean(scaled * scaled, axis=-1, keepdims=True)
            normed = (scaled * lax.rsqrt(mean_square + 1e-06) * gain[...]).astype(jnp.bfloat16)
            mixed = dot32(normed, w_mix[...])
            enc[b, :, t * BLK : (t + 1) * BLK] = (
                own[t, b].astype(jnp.float32) + silu(mixed)
            ).astype(jnp.bfloat16)
        lanes = slice(b * BLK, (b + 1) * BLK)
        rows = lax.broadcasted_iota(jnp.int32, (coarse, BLK), 0)
        pooling = jnp.where(
            rows == cluster_row[:, lanes], weight_row[:, lanes], 0.0
        ).astype(jnp.bfloat16)
        pooled = pooled + dot32(pooling, enc[b])
    pooled = pooled.astype(jnp.bfloat16)
    owner_hot = (
        lax.broadcasted_iota(jnp.int32, (devices, coarse), 0) == owner_row[...]
    ).astype(jnp.float32).astype(jnp.bfloat16)
    bases = []
    for t in range(steps):
        piece = pooled[:, t * BLK : (t + 1) * BLK]
        lifted = silu(dot32(piece, w_coarse[...])).astype(jnp.bfloat16)
        partial_ref[t] = dot32(owner_hot, lifted)
        bases.append((piece.astype(jnp.float32) + lifted.astype(jnp.float32)).astype(jnp.bfloat16))
    base = jnp.concatenate(bases, axis=1)
    for b in range(GB * GB):
        hot = (
            lax.broadcasted_iota(jnp.int32, (BLK, coarse), 1)
            == cluster_col[b * BLK : (b + 1) * BLK, :]
        ).astype(jnp.float32).astype(jnp.bfloat16)
        u = (enc[b].astype(jnp.float32) + dot32(hot, base)).astype(jnp.bfloat16)
        for t in range(steps):
            u_ref[t, b] = u[:, t * BLK : (t + 1) * BLK]


def decode_kernel(
    index,
    own,
    rx_lo,
    rx_hi,
    ry_lo,
    ry_hi,
    co_lo,
    co_hi,
    adjacency,
    region,
    owner_ext,
    w_region,
    w_out,
    *rest,
):
    out_ref, ext = rest[-2:]
    steps = own.shape[0]
    devices = region.shape[1]
    reaches = []
    for t in range(steps):
        reaches.append(dot32(region[t], w_region[...]).astype(jnp.bfloat16))
    reach = jnp.concatenate(reaches, axis=1)
    for p, (ref, k) in enumerate(
        extended_sources(own, rx_lo, rx_hi, ry_lo, ry_hi, co_lo, co_hi)
    ):
        hot = (
            lax.broadcasted_iota(jnp.int32, (BLK, devices), 1)
            == owner_ext[p * BLK : (p + 1) * BLK, :]
        ).astype(jnp.float32).astype(jnp.bfloat16)
        added = dot32(hot, reach)
        for t in range(steps):
            lanes = slice(t * BLK, (t + 1) * BLK)
            ext[p, :, lanes] = (ref[t, k].astype(jnp.float32) + added[:, lanes]).astype(
                jnp.bfloat16
            )
    for b in range(GB * GB):
        second = diffuse_block(b, index, adjacency, ext).astype(jnp.bfloat16)
        centre = (b // GB + 1) * SIDE + b % GB + 1
        for t in range(steps):
            lanes = slice(t * BLK, (t + 1) * BLK)
            mixed = dot32(second[:, lanes], w_out[...])
            out_ref[t, b] = (ext[centre, :, lanes].astype(jnp.float32) + silu(mixed)).astype(
                jnp.bfloat16
            )


def stepped(array, per, offset=0):
    tail = array.shape[1:]
    zeros = (0,) * len(tail)
    return pl.BlockSpec((per,) + tail, lambda i, _: (i + offset,) + zeros)


def whole(array):
    zeros = (0,) * array.ndim
    return pl.BlockSpec(array.shape, lambda i, _: zeros)


def shifted(value, axis, up):
    count = lax.axis_size(axis)
    pairs = [(i, i + 1) if up else (i + 1, i) for i in range(count - 1)]
    return lax.ppermute(value, axis, pairs)


def nothing(*arrays):
    return sum(array.reshape(-1)[0].astype(jnp.float32) * 0.0 for array in arrays)


def halo(field, gate=None):
    steps = field.shape[0]
    square = field.reshape(steps, GB, GB, BLK, BLK)
    sends = [square[:, :, GB - 1], square[:, :, 0], square[:, GB - 1], square[:, 0]]
    if gate is not None:
        sends = [(send.astype(jnp.float32) + gate).astype(send.dtype) for send in sends]
    ry_lo = shifted(sends[0], "ry", True)
    ry_hi = shifted(sends[1], "ry", False)
    rx_lo = shifted(sends[2], "rx", True)
    rx_hi = shifted(sends[3], "rx", False)
    co_lo = shifted(jnp.stack([ry_lo[:, GB - 1], ry_hi[:, GB - 1]], axis=1), "rx", True)
    co_hi = shifted(jnp.stack([ry_lo[:, 0], ry_hi[:, 0]], axis=1), "rx", False)
    return rx_lo, rx_hi, ry_lo, ry_hi, co_lo, co_hi


def on_device(
    noisy_input,
    adjacency,
    neighbours,
    norm_gain,
    w_mix,
    pool_weight,
    cluster,
    owner_ids,
    w_coarse,
    w_region,
    w_out,
):
    node_rows, steps_count, channels = noisy_input.shape
    coarse = owner_ids.shape[0]
    row_devices = lax.axis_size("rx")
    col_devices = lax.axis_size("ry")
    devices = row_devices * col_devices
    blocks = GB * GB
    noisy = noisy_input.transpose(1, 0, 2).reshape(steps_count, blocks, BLK, channels)
    positions = jnp.arange(blocks, dtype=jnp.int32)
    index = (
        (positions // GB)[:, None] + neighbours // 3
    ) * SIDE + (positions % GB)[:, None] + neighbours % 3
    index = index.reshape(-1)

    targets = owner_ids[:, 0]
    owner_of = jnp.sum(
        jnp.where(
            cluster[:, None] == jnp.arange(coarse, dtype=jnp.int32)[None, :], targets[None, :], 0
        ),
        axis=1,
    )
    chunk = steps_count // CHUNKS
    per = LANES_STEPS
    grid = chunk // per
    gain = norm_gain.reshape(1, channels)
    weight_row = pool_weight.astype(jnp.float32).reshape(1, node_rows)
    cluster_row = cluster.reshape(1, node_rows)
    cluster_col = cluster.reshape(node_rows, 1)
    owner_row = targets.reshape(1, coarse)
    ext_scratch = pltpu.VMEM((SIDE * SIDE, BLK, per * BLK), jnp.bfloat16)
    params = pltpu.CompilerParams(vmem_limit_bytes=48 * 1024 * 1024)
    cost = pl.CostEstimate(flops=5_000_000_000 // CHUNKS, bytes_accessed=16_000_000 // CHUNKS, transcendentals=0)

    first = []
    for c in range(CHUNKS):
        gate = nothing(*first[-1][2:4]) if first else None
        first.append(halo(noisy[c * chunk : (c + 1) * chunk], gate))
    fields, sums, second = [], [], []
    for c in range(CHUNKS):
        constants = (
            adjacency, gain, w_mix, weight_row, cluster_row, cluster_col, owner_row, w_coarse,
        )
        u, partial = pl.pallas_call(
            encode_kernel,
            grid_spec=pltpu.PrefetchScalarGridSpec(
                num_scalar_prefetch=1,
                grid=(grid,),
                in_specs=[stepped(noisy, per, c * grid)]
                + [stepped(part, per) for part in first[c]]
                + [whole(part) for part in constants],
                out_specs=[
                    pl.BlockSpec((per, blocks, BLK, channels), lambda i, _: (i, 0, 0, 0)),
                    pl.BlockSpec((per, devices, channels), lambda i, _: (i, 0, 0)),
                ],
                scratch_shapes=[
                    ext_scratch,
                    pltpu.VMEM((blocks, BLK, per * BLK), jnp.bfloat16),
                ],
            ),
            out_shape=[
                jax.ShapeDtypeStruct((chunk, blocks, BLK, channels), jnp.bfloat16),
                jax.ShapeDtypeStruct((chunk, devices, channels), jnp.float32),
            ],
            compiler_params=params,
            cost_estimate=cost,
            name="encode",
        )(index, noisy, *first[c], *constants)
        fields.append(u)
        sums.append(partial)
        second.append(halo(u))
    marks = (owner_of + 1).reshape(GB, GB, BLK) + nothing(sums[0]).astype(jnp.int32)
    marks = jnp.concatenate(
        [shifted(marks[:, -1:], "ry", True), marks, shifted(marks[:, :1], "ry", False)], axis=1
    )
    marks = jnp.concatenate(
        [shifted(marks[-1:], "rx", True), marks, shifted(marks[:1], "rx", False)], axis=0
    )
    owner_ext = (marks - 1).reshape(SIDE * SIDE * BLK, 1)

    gate = nothing(*second[0][4:6])
    mine = lax.all_to_all(
        jnp.concatenate(sums, axis=0).transpose(1, 0, 2) + gate,
        ("rx", "ry"),
        split_axis=0,
        concat_axis=0,
        tiled=True,
    )
    own_region = (jnp.sum(mine, axis=0) / float(coarse)).astype(jnp.bfloat16)
    region = lax.all_to_all(
        jnp.broadcast_to(own_region[None], (devices, steps_count, channels)),
        ("rx", "ry"),
        split_axis=0,
        concat_axis=0,
        tiled=True,
    ).transpose(1, 0, 2)

    out = None
    for c in range(CHUNKS):
        shared = (owner_ext, w_region, w_out)
        extra = () if out is None else (out,)
        operands = (index, fields[c], *second[c], adjacency, region, *shared, *extra)
        out = pl.pallas_call(
            decode_kernel,
            grid_spec=pltpu.PrefetchScalarGridSpec(
                num_scalar_prefetch=1,
                grid=(grid,),
                in_specs=[stepped(fields[c], per)]
                + [stepped(part, per) for part in second[c]]
                + [whole(adjacency), stepped(region, per, c * grid)]
                + [whole(part) for part in shared]
                + [pl.BlockSpec(memory_space=pl.ANY)] * len(extra),
                out_specs=pl.BlockSpec(
                    (per, blocks, BLK, channels), lambda i, _, c=c: (i + c * grid, 0, 0, 0)
                ),
                scratch_shapes=[ext_scratch],
            ),
            out_shape=jax.ShapeDtypeStruct((steps_count, blocks, BLK, channels), jnp.bfloat16),
            input_output_aliases={len(operands) - 1: 0} if extra else {},
            compiler_params=params,
            cost_estimate=cost,
            name="decode",
        )(*operands)
    return out.reshape(steps_count, node_rows, channels).transpose(1, 0, 2)


def solution(mesh):
    in_specs = (
        P(("rx", "ry"), None, None),
        P(("rx", "ry"), None, None, None),
        P(("rx", "ry"), None),
        P(),
        P(),
        P(("rx", "ry")),
        P(("rx", "ry")),
        P(("rx", "ry"), None),
        P(),
        P(),
        P(),
    )
    out_specs = P(("rx", "ry"), None, None)
    return jax.shard_map(
        on_device, mesh=mesh, in_specs=in_specs, out_specs=out_specs, check_vma=False
    )
```

```python
import jax
import jax.numpy as jnp
from jax import lax
from jax.experimental import pallas as pl
from jax.experimental.pallas import tpu as pltpu
from jax.sharding import PartitionSpec as P

GB = 3
BLK = 128
SIDE = GB + 2
CHUNKS = 2
LANES_STEPS = 2


def silu(v):
    return v / (1.0 + jnp.exp(-v))


def dot32(a, b):
    return jnp.dot(a, b, preferred_element_type=jnp.float32)


def extended_sources(own, rx_lo, rx_hi, ry_lo, ry_hi):
    sources = []
    for r in range(SIDE):
        for c in range(SIDE):
            if r in (0, SIDE - 1):
                sources.append((rx_lo if r == 0 else rx_hi, c))
            elif c in (0, SIDE - 1):
                sources.append((ry_lo if c == 0 else ry_hi, r - 1))
            else:
                sources.append((own, (r - 1) * GB + c - 1))
    return sources


def diffuse_block(b, index, adjacency, ext):
    lhs = jnp.concatenate([adjacency[b, n] for n in range(adjacency.shape[1])], axis=1)
    rhs = jnp.concatenate(
        [ext[index[b * adjacency.shape[1] + n]] for n in range(adjacency.shape[1])], axis=0
    )
    return dot32(lhs, rhs)


def encode_kernel(
    index,
    own,
    rx_lo,
    rx_hi,
    ry_lo,
    ry_hi,
    adjacency,
    gain,
    w_mix,
    weight_row,
    cluster_row,
    cluster_col,
    owner_row,
    w_coarse,
    u_ref,
    left_ref,
    right_ref,
    partial_ref,
    ext,
    enc,
):
    steps = own.shape[0]
    coarse = owner_row.shape[1]
    nodes = cluster_row.shape[1]
    devices = partial_ref.shape[1]
    for p, (ref, k) in enumerate(
        extended_sources(own, rx_lo, rx_hi, ry_lo, ry_hi)
    ):
        for t in range(steps):
            ext[p, :, t * BLK : (t + 1) * BLK] = ref[t, k]
    pooled = jnp.zeros((coarse, steps * BLK), jnp.float32)
    for b in range(GB * GB):
        summed = diffuse_block(b, index, adjacency, ext)
        for t in range(steps):
            scaled = summed[:, t * BLK : (t + 1) * BLK].astype(jnp.bfloat16).astype(jnp.float32)
            mean_square = jnp.mean(scaled * scaled, axis=-1, keepdims=True)
            normed = (scaled * lax.rsqrt(mean_square + 1e-06) * gain[...]).astype(jnp.bfloat16)
            mixed = dot32(normed, w_mix[...])
            enc[b, :, t * BLK : (t + 1) * BLK] = (
                own[t, b].astype(jnp.float32) + silu(mixed)
            ).astype(jnp.bfloat16)
        lanes = slice(b * BLK, (b + 1) * BLK)
        rows = lax.broadcasted_iota(jnp.int32, (coarse, BLK), 0)
        pooling = jnp.where(
            rows == cluster_row[:, lanes], weight_row[:, lanes], 0.0
        ).astype(jnp.bfloat16)
        pooled = pooled + dot32(pooling, enc[b])
    pooled = pooled.astype(jnp.bfloat16)
    owner_hot = (
        lax.broadcasted_iota(jnp.int32, (devices, coarse), 0) == owner_row[...]
    ).astype(jnp.float32).astype(jnp.bfloat16)
    bases = []
    for t in range(steps):
        piece = pooled[:, t * BLK : (t + 1) * BLK]
        lifted = silu(dot32(piece, w_coarse[...])).astype(jnp.bfloat16)
        partial_ref[t] = dot32(owner_hot, lifted)
        bases.append((piece.astype(jnp.float32) + lifted.astype(jnp.float32)).astype(jnp.bfloat16))
    base = jnp.concatenate(bases, axis=1)
    for b in range(GB * GB):
        hot = (
            lax.broadcasted_iota(jnp.int32, (BLK, coarse), 1)
            == cluster_col[b * BLK : (b + 1) * BLK, :]
        ).astype(jnp.float32).astype(jnp.bfloat16)
        u = (enc[b].astype(jnp.float32) + dot32(hot, base)).astype(jnp.bfloat16)
        for t in range(steps):
            piece = u[:, t * BLK : (t + 1) * BLK]
            u_ref[t, b] = piece
            if b % GB == 0:
                left_ref[t, b // GB] = piece
            if b % GB == GB - 1:
                right_ref[t, b // GB] = piece


def decode_kernel(
    index,
    own,
    rx_lo,
    rx_hi,
    ry_lo,
    ry_hi,
    adjacency,
    region,
    owner_ext,
    w_region,
    w_out,
    *rest,
):
    out_ref, ext = rest[-2:]
    steps = own.shape[0]
    devices = region.shape[1]
    reaches = []
    for t in range(steps):
        reaches.append(dot32(region[t], w_region[...]).astype(jnp.bfloat16))
    reach = jnp.concatenate(reaches, axis=1)
    for p, (ref, k) in enumerate(
        extended_sources(own, rx_lo, rx_hi, ry_lo, ry_hi)
    ):
        hot = (
            lax.broadcasted_iota(jnp.int32, (BLK, devices), 1)
            == owner_ext[p * BLK : (p + 1) * BLK, :]
        ).astype(jnp.float32).astype(jnp.bfloat16)
        added = dot32(hot, reach)
        for t in range(steps):
            lanes = slice(t * BLK, (t + 1) * BLK)
            ext[p, :, lanes] = (ref[t, k].astype(jnp.float32) + added[:, lanes]).astype(
                jnp.bfloat16
            )
    for b in range(GB * GB):
        second = diffuse_block(b, index, adjacency, ext).astype(jnp.bfloat16)
        centre = (b // GB + 1) * SIDE + b % GB + 1
        for t in range(steps):
            lanes = slice(t * BLK, (t + 1) * BLK)
            mixed = dot32(second[:, lanes], w_out[...])
            out_ref[t, b] = (ext[centre, :, lanes].astype(jnp.float32) + silu(mixed)).astype(
                jnp.bfloat16
            )


def stepped(array, per, offset=0):
    tail = array.shape[1:]
    zeros = (0,) * len(tail)
    return pl.BlockSpec((per,) + tail, lambda i, _: (i + offset,) + zeros)


def whole(array):
    zeros = (0,) * array.ndim
    return pl.BlockSpec(array.shape, lambda i, _: zeros)


def shifted(value, axis, up):
    count = lax.axis_size(axis)
    pairs = [(i, i + 1) if up else (i + 1, i) for i in range(count - 1)]
    return lax.ppermute(value, axis, pairs)


def nothing(*arrays):
    return sum(array.reshape(-1)[0].astype(jnp.float32) * 0.0 for array in arrays)


def gated(value, gate):
    return value if gate is None else (value.astype(jnp.float32) + gate).astype(value.dtype)


def columns(left, right, gate=None):
    return shifted(gated(right, gate), "ry", True), shifted(gated(left, gate), "ry", False)


def rows(field, ry_lo, ry_hi, gate=None):
    def wide(row):
        middle = field[:, row * GB : (row + 1) * GB]
        line = [ry_lo[:, row : row + 1], middle, ry_hi[:, row : row + 1]]
        return gated(jnp.concatenate(line, axis=1), gate)

    return shifted(wide(GB - 1), "rx", True), shifted(wide(0), "rx", False)


def on_device(
    noisy_input,
    adjacency,
    neighbours,
    norm_gain,
    w_mix,
    pool_weight,
    cluster,
    owner_ids,
    w_coarse,
    w_region,
    w_out,
):
    node_rows, steps_count, channels = noisy_input.shape
    coarse = owner_ids.shape[0]
    row_devices = lax.axis_size("rx")
    col_devices = lax.axis_size("ry")
    devices = row_devices * col_devices
    blocks = GB * GB
    noisy = noisy_input.transpose(1, 0, 2).reshape(steps_count, blocks, BLK, channels)
    positions = jnp.arange(blocks, dtype=jnp.int32)
    index = (
        (positions // GB)[:, None] + neighbours // 3
    ) * SIDE + (positions % GB)[:, None] + neighbours % 3
    index = index.reshape(-1)

    targets = owner_ids[:, 0]
    owner_of = jnp.sum(
        jnp.where(
            cluster[:, None] == jnp.arange(coarse, dtype=jnp.int32)[None, :], targets[None, :], 0
        ),
        axis=1,
    )
    ext_rows = jnp.arange(SIDE * SIDE, dtype=jnp.int32)
    grid_row = lax.axis_index("rx") * GB + ext_rows // SIDE - 1
    grid_col = lax.axis_index("ry") * GB + ext_rows % SIDE - 1
    inside = (
        (grid_row >= 0)
        & (grid_row < row_devices * GB)
        & (grid_col >= 0)
        & (grid_col < col_devices * GB)
    )
    grid_row = jnp.clip(grid_row, 0, row_devices * GB - 1)
    grid_col = jnp.clip(grid_col, 0, col_devices * GB - 1)
    place = (
        (grid_row // GB * col_devices + grid_col // GB) * blocks
        + grid_row % GB * GB
        + grid_col % GB
    )

    chunk = steps_count // CHUNKS
    per = LANES_STEPS
    grid = chunk // per
    gain = norm_gain.reshape(1, channels)
    weight_row = pool_weight.astype(jnp.float32).reshape(1, node_rows)
    cluster_row = cluster.reshape(1, node_rows)
    cluster_col = cluster.reshape(node_rows, 1)
    owner_row = targets.reshape(1, coarse)
    ext_scratch = pltpu.VMEM((SIDE * SIDE, BLK, per * BLK), jnp.bfloat16)
    params = pltpu.CompilerParams(vmem_limit_bytes=48 * 1024 * 1024)
    cost = pl.CostEstimate(flops=5_000_000_000 // CHUNKS, bytes_accessed=16_000_000 // CHUNKS, transcendentals=0)

    first = []
    for c in range(CHUNKS):
        gate = nothing(*first[-1][2:4]) if first else None
        field = noisy[c * chunk : (c + 1) * chunk]
        sides = columns(field[:, 0::GB], field[:, GB - 1 :: GB], gate)
        first.append((*rows(field, *sides), *sides))
    fields, sums, second = [], [], []
    for c in range(CHUNKS):
        constants = (
            adjacency, gain, w_mix, weight_row, cluster_row, cluster_col, owner_row, w_coarse,
        )
        u, left, right, partial = pl.pallas_call(
            encode_kernel,
            grid_spec=pltpu.PrefetchScalarGridSpec(
                num_scalar_prefetch=1,
                grid=(grid,),
                in_specs=[stepped(noisy, per, c * grid)]
                + [stepped(part, per) for part in first[c]]
                + [whole(part) for part in constants],
                out_specs=[
                    pl.BlockSpec((per, blocks, BLK, channels), lambda i, _: (i, 0, 0, 0)),
                    pl.BlockSpec((per, GB, BLK, channels), lambda i, _: (i, 0, 0, 0)),
                    pl.BlockSpec((per, GB, BLK, channels), lambda i, _: (i, 0, 0, 0)),
                    pl.BlockSpec((per, devices, channels), lambda i, _: (i, 0, 0)),
                ],
                scratch_shapes=[
                    ext_scratch,
                    pltpu.VMEM((blocks, BLK, per * BLK), jnp.bfloat16),
                ],
            ),
            out_shape=[
                jax.ShapeDtypeStruct((chunk, blocks, BLK, channels), jnp.bfloat16),
                jax.ShapeDtypeStruct((chunk, GB, BLK, channels), jnp.bfloat16),
                jax.ShapeDtypeStruct((chunk, GB, BLK, channels), jnp.bfloat16),
                jax.ShapeDtypeStruct((chunk, devices, channels), jnp.float32),
            ],
            compiler_params=params,
            cost_estimate=cost,
            name="encode",
        )(index, noisy, *first[c], *constants)
        fields.append(u)
        sums.append(partial)
        second.append(columns(left, right))
    for c in range(CHUNKS):
        gate = nothing(sums[-1]) if c + 1 < CHUNKS else None
        second[c] = (*rows(fields[c], *second[c], gate), *second[c])
    gate = nothing(*second[0][2:4])
    mine = lax.all_to_all(
        jnp.concatenate(sums, axis=0).transpose(1, 0, 2) + gate,
        ("rx", "ry"),
        split_axis=0,
        concat_axis=0,
        tiled=True,
    )
    own_region = (jnp.sum(mine, axis=0) / float(coarse)).astype(jnp.bfloat16)
    told = jnp.concatenate([own_region, owner_of.reshape(blocks, BLK).astype(jnp.bfloat16)], axis=0)
    told = lax.all_to_all(
        jnp.broadcast_to(told[None], (devices,) + told.shape),
        ("rx", "ry"),
        split_axis=0,
        concat_axis=0,
        tiled=True,
    )
    region = told[:, :steps_count].transpose(1, 0, 2)
    everyone = told[:, steps_count:].reshape(devices * blocks, BLK)
    owner_ext = jnp.where(inside[:, None], everyone[place].astype(jnp.int32), -1)
    owner_ext = owner_ext.reshape(SIDE * SIDE * BLK, 1)

    out = None
    for c in range(CHUNKS):
        shared = (owner_ext, w_region, w_out)
        extra = () if out is None else (out,)
        operands = (index, fields[c], *second[c], adjacency, region, *shared, *extra)
        out = pl.pallas_call(
            decode_kernel,
            grid_spec=pltpu.PrefetchScalarGridSpec(
                num_scalar_prefetch=1,
                grid=(grid,),
                in_specs=[stepped(fields[c], per)]
                + [stepped(part, per) for part in second[c]]
                + [whole(adjacency), stepped(region, per, c * grid)]
                + [whole(part) for part in shared]
                + [pl.BlockSpec(memory_space=pl.ANY)] * len(extra),
                out_specs=pl.BlockSpec(
                    (per, blocks, BLK, channels), lambda i, _, c=c: (i + c * grid, 0, 0, 0)
                ),
                scratch_shapes=[ext_scratch],
            ),
            out_shape=jax.ShapeDtypeStruct((steps_count, blocks, BLK, channels), jnp.bfloat16),
            input_output_aliases={len(operands) - 1: 0} if extra else {},
            compiler_params=params,
            cost_estimate=cost,
            name="decode",
        )(*operands)
    return out.reshape(steps_count, node_rows, channels).transpose(1, 0, 2)


def solution(mesh):
    in_specs = (
        P(("rx", "ry"), None, None),
        P(("rx", "ry"), None, None, None),
        P(("rx", "ry"), None),
        P(),
        P(),
        P(("rx", "ry")),
        P(("rx", "ry")),
        P(("rx", "ry"), None),
        P(),
        P(),
        P(),
    )
    out_specs = P(("rx", "ry"), None, None)
    return jax.shard_map(
        on_device, mesh=mesh, in_specs=in_specs, out_specs=out_specs, check_vma=False
    )
```

```python
import jax
import jax.numpy as jnp
from jax import lax
from jax.experimental import pallas as pl
from jax.experimental.pallas import tpu as pltpu
from jax.sharding import PartitionSpec as P

GB = 3
BLK = 128
SIDE = GB + 2
CHUNKS = 2
LANES_STEPS = 2


def silu(v):
    return v / (1.0 + jnp.exp(-v))


def dot32(a, b):
    return jnp.dot(a, b, preferred_element_type=jnp.float32)


def extended_sources(own, rx_lo, rx_hi, ry_lo, ry_hi, co_lo, co_hi):
    sources = []
    for r in range(SIDE):
        for c in range(SIDE):
            if r in (0, SIDE - 1):
                row, corner = (rx_lo, co_lo) if r == 0 else (rx_hi, co_hi)
                if c in (0, SIDE - 1):
                    sources.append((corner, 0 if c == 0 else 1))
                else:
                    sources.append((row, c - 1))
            elif c in (0, SIDE - 1):
                sources.append((ry_lo if c == 0 else ry_hi, r - 1))
            else:
                sources.append((own, (r - 1) * GB + c - 1))
    return sources


def diffuse_block(b, index, adjacency, ext):
    lhs = jnp.concatenate([adjacency[b, n] for n in range(adjacency.shape[1])], axis=1)
    rhs = jnp.concatenate(
        [ext[index[b * adjacency.shape[1] + n]] for n in range(adjacency.shape[1])], axis=0
    )
    return dot32(lhs, rhs)


def encode_kernel(
    index,
    own,
    rx_lo,
    rx_hi,
    ry_lo,
    ry_hi,
    co_lo,
    co_hi,
    adjacency,
    gain,
    w_mix,
    weight_row,
    cluster_row,
    cluster_col,
    owner_row,
    w_coarse,
    u_ref,
    partial_ref,
    ext,
    enc,
):
    steps = own.shape[0]
    coarse = owner_row.shape[1]
    nodes = cluster_row.shape[1]
    devices = partial_ref.shape[1]
    for p, (ref, k) in enumerate(
        extended_sources(own, rx_lo, rx_hi, ry_lo, ry_hi, co_lo, co_hi)
    ):
        for t in range(steps):
            ext[p, :, t * BLK : (t + 1) * BLK] = ref[t, k]
    pooled = jnp.zeros((coarse, steps * BLK), jnp.float32)
    for b in range(GB * GB):
        summed = diffuse_block(b, index, adjacency, ext)
        for t in range(steps):
            scaled = summed[:, t * BLK : (t + 1) * BLK].astype(jnp.bfloat16).astype(jnp.float32)
            mean_square = jnp.mean(scaled * scaled, axis=-1, keepdims=True)
            normed = (scaled * lax.rsqrt(mean_square + 1e-06) * gain[...]).astype(jnp.bfloat16)
            mixed = dot32(normed, w_mix[...])
            enc[b, :, t * BLK : (t + 1) * BLK] = (
                own[t, b].astype(jnp.float32) + silu(mixed)
            ).astype(jnp.bfloat16)
        lanes = slice(b * BLK, (b + 1) * BLK)
        rows = lax.broadcasted_iota(jnp.int32, (coarse, BLK), 0)
        pooling = jnp.where(
            rows == cluster_row[:, lanes], weight_row[:, lanes], 0.0
        ).astype(jnp.bfloat16)
        pooled = pooled + dot32(pooling, enc[b])
    pooled = pooled.astype(jnp.bfloat16)
    owner_hot = (
        lax.broadcasted_iota(jnp.int32, (devices, coarse), 0) == owner_row[...]
    ).astype(jnp.float32).astype(jnp.bfloat16)
    bases = []
    for t in range(steps):
        piece = pooled[:, t * BLK : (t + 1) * BLK]
        lifted = silu(dot32(piece, w_coarse[...])).astype(jnp.bfloat16)
        partial_ref[t] = dot32(owner_hot, lifted)
        bases.append((piece.astype(jnp.float32) + lifted.astype(jnp.float32)).astype(jnp.bfloat16))
    base = jnp.concatenate(bases, axis=1)
    for b in range(GB * GB):
        hot = (
            lax.broadcasted_iota(jnp.int32, (BLK, coarse), 1)
            == cluster_col[b * BLK : (b + 1) * BLK, :]
        ).astype(jnp.float32).astype(jnp.bfloat16)
        u = (enc[b].astype(jnp.float32) + dot32(hot, base)).astype(jnp.bfloat16)
        for t in range(steps):
            u_ref[t, b] = u[:, t * BLK : (t + 1) * BLK]


def decode_kernel(
    index,
    own,
    rx_lo,
    rx_hi,
    ry_lo,
    ry_hi,
    co_lo,
    co_hi,
    adjacency,
    region,
    owner_ext,
    w_region,
    w_out,
    *rest,
):
    out_ref, ext = rest[-2:]
    steps = own.shape[0]
    devices = region.shape[1]
    reaches = []
    for t in range(steps):
        reaches.append(dot32(region[t], w_region[...]).astype(jnp.bfloat16))
    reach = jnp.concatenate(reaches, axis=1)
    for p, (ref, k) in enumerate(
        extended_sources(own, rx_lo, rx_hi, ry_lo, ry_hi, co_lo, co_hi)
    ):
        hot = (
            lax.broadcasted_iota(jnp.int32, (BLK, devices), 1)
            == owner_ext[p * BLK : (p + 1) * BLK, :]
        ).astype(jnp.float32).astype(jnp.bfloat16)
        added = dot32(hot, reach)
        for t in range(steps):
            lanes = slice(t * BLK, (t + 1) * BLK)
            ext[p, :, lanes] = (ref[t, k].astype(jnp.float32) + added[:, lanes]).astype(
                jnp.bfloat16
            )
    for b in range(GB * GB):
        second = diffuse_block(b, index, adjacency, ext).astype(jnp.bfloat16)
        centre = (b // GB + 1) * SIDE + b % GB + 1
        for t in range(steps):
            lanes = slice(t * BLK, (t + 1) * BLK)
            mixed = dot32(second[:, lanes], w_out[...])
            out_ref[t, b] = (ext[centre, :, lanes].astype(jnp.float32) + silu(mixed)).astype(
                jnp.bfloat16
            )


def stepped(array, per, offset=0):
    tail = array.shape[1:]
    zeros = (0,) * len(tail)
    return pl.BlockSpec((per,) + tail, lambda i, _: (i + offset,) + zeros)


def whole(array):
    zeros = (0,) * array.ndim
    return pl.BlockSpec(array.shape, lambda i, _: zeros)


def shifted(value, axis, up):
    count = lax.axis_size(axis)
    pairs = [(i, i + 1) if up else (i + 1, i) for i in range(count - 1)]
    return lax.ppermute(value, axis, pairs)


def nothing(*arrays):
    return sum(array.reshape(-1)[0].astype(jnp.float32) * 0.0 for array in arrays)


def halo(field, gate=None):
    steps = field.shape[0]
    square = field.reshape(steps, GB, GB, BLK, BLK)
    sends = [square[:, :, GB - 1], square[:, :, 0], square[:, GB - 1], square[:, 0]]
    if gate is not None:
        sends = [(send.astype(jnp.float32) + gate).astype(send.dtype) for send in sends]
    ry_lo = shifted(sends[0], "ry", True)
    ry_hi = shifted(sends[1], "ry", False)
    rx_lo = shifted(sends[2], "rx", True)
    rx_hi = shifted(sends[3], "rx", False)
    co_lo = shifted(jnp.stack([ry_lo[:, GB - 1], ry_hi[:, GB - 1]], axis=1), "rx", True)
    co_hi = shifted(jnp.stack([ry_lo[:, 0], ry_hi[:, 0]], axis=1), "rx", False)
    return rx_lo, rx_hi, ry_lo, ry_hi, co_lo, co_hi


def on_device(
    noisy_input,
    adjacency,
    neighbours,
    norm_gain,
    w_mix,
    pool_weight,
    cluster,
    owner_ids,
    w_coarse,
    w_region,
    w_out,
):
    node_rows, steps_count, channels = noisy_input.shape
    coarse = owner_ids.shape[0]
    row_devices = lax.axis_size("rx")
    col_devices = lax.axis_size("ry")
    devices = row_devices * col_devices
    blocks = GB * GB
    noisy = noisy_input.transpose(1, 0, 2).reshape(steps_count, blocks, BLK, channels)
    positions = jnp.arange(blocks, dtype=jnp.int32)
    index = (
        (positions // GB)[:, None] + neighbours // 3
    ) * SIDE + (positions % GB)[:, None] + neighbours % 3
    index = index.reshape(-1)

    targets = owner_ids[:, 0]
    owner_of = jnp.sum(
        jnp.where(
            cluster[:, None] == jnp.arange(coarse, dtype=jnp.int32)[None, :], targets[None, :], 0
        ),
        axis=1,
    )
    ext_rows = jnp.arange(SIDE * SIDE, dtype=jnp.int32)
    grid_row = lax.axis_index("rx") * GB + ext_rows // SIDE - 1
    grid_col = lax.axis_index("ry") * GB + ext_rows % SIDE - 1
    inside = (
        (grid_row >= 0)
        & (grid_row < row_devices * GB)
        & (grid_col >= 0)
        & (grid_col < col_devices * GB)
    )
    grid_row = jnp.clip(grid_row, 0, row_devices * GB - 1)
    grid_col = jnp.clip(grid_col, 0, col_devices * GB - 1)
    place = (
        (grid_row // GB * col_devices + grid_col // GB) * blocks
        + grid_row % GB * GB
        + grid_col % GB
    )

    chunk = steps_count // CHUNKS
    per = LANES_STEPS
    grid = chunk // per
    gain = norm_gain.reshape(1, channels)
    weight_row = pool_weight.astype(jnp.float32).reshape(1, node_rows)
    cluster_row = cluster.reshape(1, node_rows)
    cluster_col = cluster.reshape(node_rows, 1)
    owner_row = targets.reshape(1, coarse)
    ext_scratch = pltpu.VMEM((SIDE * SIDE, BLK, per * BLK), jnp.bfloat16)
    params = pltpu.CompilerParams(vmem_limit_bytes=48 * 1024 * 1024)
    cost = pl.CostEstimate(flops=5_000_000_000 // CHUNKS, bytes_accessed=16_000_000 // CHUNKS, transcendentals=0)

    first = []
    for c in range(CHUNKS):
        gate = nothing(*first[-1][2:4]) if first else None
        first.append(halo(noisy[c * chunk : (c + 1) * chunk], gate))
    fields, sums, second = [], [], []
    for c in range(CHUNKS):
        constants = (
            adjacency, gain, w_mix, weight_row, cluster_row, cluster_col, owner_row, w_coarse,
        )
        u, partial = pl.pallas_call(
            encode_kernel,
            grid_spec=pltpu.PrefetchScalarGridSpec(
                num_scalar_prefetch=1,
                grid=(grid,),
                in_specs=[stepped(noisy, per, c * grid)]
                + [stepped(part, per) for part in first[c]]
                + [whole(part) for part in constants],
                out_specs=[
                    pl.BlockSpec((per, blocks, BLK, channels), lambda i, _: (i, 0, 0, 0)),
                    pl.BlockSpec((per, devices, channels), lambda i, _: (i, 0, 0)),
                ],
                scratch_shapes=[
                    ext_scratch,
                    pltpu.VMEM((blocks, BLK, per * BLK), jnp.bfloat16),
                ],
            ),
            out_shape=[
                jax.ShapeDtypeStruct((chunk, blocks, BLK, channels), jnp.bfloat16),
                jax.ShapeDtypeStruct((chunk, devices, channels), jnp.float32),
            ],
            compiler_params=params,
            cost_estimate=cost,
            name="encode",
        )(index, noisy, *first[c], *constants)
        fields.append(u)
        sums.append(partial)
        second.append(halo(u))
    gate = nothing(*second[0][4:6])
    mine = lax.all_to_all(
        jnp.concatenate(sums, axis=0).transpose(1, 0, 2) + gate,
        ("rx", "ry"),
        split_axis=0,
        concat_axis=0,
        tiled=True,
    )
    own_region = (jnp.sum(mine, axis=0) / float(coarse)).astype(jnp.bfloat16)
    told = jnp.concatenate([own_region, owner_of.reshape(blocks, BLK).astype(jnp.bfloat16)], axis=0)
    told = lax.all_to_all(
        jnp.broadcast_to(told[None], (devices,) + told.shape),
        ("rx", "ry"),
        split_axis=0,
        concat_axis=0,
        tiled=True,
    )
    region = told[:, :steps_count].transpose(1, 0, 2)
    everyone = told[:, steps_count:].reshape(devices * blocks, BLK)
    owner_ext = jnp.where(inside[:, None], everyone[place].astype(jnp.int32), -1)
    owner_ext = owner_ext.reshape(SIDE * SIDE * BLK, 1)

    out = None
    for c in range(CHUNKS):
        shared = (owner_ext, w_region, w_out)
        extra = () if out is None else (out,)
        operands = (index, fields[c], *second[c], adjacency, region, *shared, *extra)
        out = pl.pallas_call(
            decode_kernel,
            grid_spec=pltpu.PrefetchScalarGridSpec(
                num_scalar_prefetch=1,
                grid=(grid,),
                in_specs=[stepped(fields[c], per)]
                + [stepped(part, per) for part in second[c]]
                + [whole(adjacency), stepped(region, per, c * grid)]
                + [whole(part) for part in shared]
                + [pl.BlockSpec(memory_space=pl.ANY)] * len(extra),
                out_specs=pl.BlockSpec(
                    (per, blocks, BLK, channels), lambda i, _, c=c: (i + c * grid, 0, 0, 0)
                ),
                scratch_shapes=[ext_scratch],
            ),
            out_shape=jax.ShapeDtypeStruct((steps_count, blocks, BLK, channels), jnp.bfloat16),
            input_output_aliases={len(operands) - 1: 0} if extra else {},
            compiler_params=params,
            cost_estimate=cost,
            name="decode",
        )(*operands)
    return out.reshape(steps_count, node_rows, channels).transpose(1, 0, 2)


def solution(mesh):
    in_specs = (
        P(("rx", "ry"), None, None),
        P(("rx", "ry"), None, None, None),
        P(("rx", "ry"), None),
        P(),
        P(),
        P(("rx", "ry")),
        P(("rx", "ry")),
        P(("rx", "ry"), None),
        P(),
        P(),
        P(),
    )
    out_specs = P(("rx", "ry"), None, None)
    return jax.shard_map(
        on_device, mesh=mesh, in_specs=in_specs, out_specs=out_specs, check_vma=False
    )
```
